32 devices in a mesh: grp: 4 (over y, x), blk: 8 (over z, core).
Axes of the slice: x: 2, y: 2, z: 4, core: 2. Of those that a mesh axis runs over, the one named last changes fastest.
Arguments:
- integrals: bfloat16 [4, 8, 10, 24, 128, 128], P('grp', 'blk'), may hold values from -6 to 6
- coefficients: bfloat16 [3072, 192], P('blk'), may hold values from -0.25 to 0.25
- tile_blocks: int32 [4, 8, 10, 2], P('grp', 'blk'), may hold values from 0 to 23
- block_owner: int32 [48], replicated, may hold values from 0 to 3, as said below
Outputs:
- owned: bfloat16 [96, 4, 4, 192, 192], P('grp', None, None, 'blk')
The draws below stay inside these ranges and needn't reach their ends.
Inputs may be any that keep to these rules, and one draw needn't show every extreme that they name: `block_owner`: each owner holds at most 24 ij blocks, and some owner holds exactly 24.
All inputs are finite; a program needn't handle non-finite values.
Results may differ from the reference program's by a relative error of at most 0.0049.
Values may be sent and summed in bfloat16 or wider, within the bound.
A program may use at most 64 MiB of HBM per device.

```python
import jax
import jax.numpy as jnp
from jax import lax

NMO = 192
SB = 128
NSH = 24
NBF = 3072
KT = 10
R = 24
IJB = 48
CAP = 24
IPB = 4
N_GRP = 4
N_BLK = 8


def draw_block_owner(key, part):
    key_busy = jax.random.fold_in(key, 11)
    key_perm = jax.random.fold_in(key, 12)
    key_rest = jax.random.fold_in(key, 13)
    busiest = jax.random.randint(key_busy, (), 0, N_GRP).astype(jnp.int32)
    shuffled = jax.random.permutation(key_perm, IJB).astype(jnp.int32)
    position = jnp.argsort(shuffled).astype(jnp.int32)
    others = jax.random.randint(key_rest, (IJB,), 0, N_GRP - 1).astype(jnp.int32)
    others = others + (others >= busiest).astype(jnp.int32)
    return jnp.where(position < CAP, busiest, others).astype(jnp.int32)


def place_ends(drawn, rng, smallest, largest):
    longest = drawn.shape.index(max(drawn.shape))
    spots = []
    for shift in (0, 1):
        where = [jax.random.randint(jax.random.fold_in(rng, axis), (), 0, length) for axis, length in enumerate(drawn.shape)]
        where[longest] = (where[longest] + shift) % drawn.shape[longest]
        spots.append(tuple(where))
    return drawn.at[spots[0]].set(smallest).at[spots[1]].set(largest)


def steps_of(rng, dims, shards, least, high):
    gain = 1.0
    for axis_at, blocks in shards:
        draws = jax.random.uniform(jax.random.fold_in(jax.random.fold_in(rng, 6), axis_at), (blocks,), jnp.float32, least / len(shards), high / len(shards))
        gain = gain * jnp.repeat(jnp.exp(draws), dims[axis_at] // blocks).reshape((-1,) + (1,) * (len(dims) - 1 - axis_at))
    return gain


def normal_values(own_key, dims, deviation, most, pieces=(), kind=jnp.bfloat16):
    result = jax.random.normal(own_key, dims, jnp.float32) * deviation
    if len(pieces) > 0:
        result = steps_of(own_key, dims, pieces, -0.22, 0.18) * result
    return jnp.clip(result, min=-most, max=most).astype(kind)


def setup_inputs(seed: int = 0) -> dict:
    arg_keys = jax.random.split(jax.random.key(seed), 5)
    return {
        "integrals": normal_values(arg_keys[0], (N_GRP, N_BLK, KT, R, SB, SB), 1.0, 6.0, ((0, 4), (1, 8))),
        "coefficients": normal_values(arg_keys[1], (NBF, NMO), (4 * SB) ** -0.5, 0.25, ((0, 8),)),
        "tile_blocks": place_ends(jax.random.randint(arg_keys[2], (N_GRP, N_BLK, KT, 2), 0, NSH), jax.random.fold_in(arg_keys[2], 1), 0, NSH - 1).astype(jnp.int32),
        "block_owner": draw_block_owner(jax.random.fold_in(arg_keys[4], 71), 0),
    }


def slot_table(block_owner, groups, capacity):
    count = block_owner.shape[0]
    order = jnp.arange(count, dtype=jnp.int32)
    same = block_owner[:, None] == block_owner[None, :]
    earlier = order[None, :] < order[:, None]
    rank = jnp.sum((same & earlier).astype(jnp.int32), axis=1).astype(jnp.int32)
    slot = (block_owner * capacity + rank).astype(jnp.int32)
    slots = jnp.arange(groups * capacity, dtype=jnp.int32)
    match = slot[None, :] == slots[:, None]
    source = jnp.sum(jnp.where(match, order[None, :], 0), axis=1).astype(jnp.int32)
    filled = jnp.any(match, axis=1)
    return source, filled


def one_device(args):
    tiles, blocks, panels = args
    la_coef = jnp.take(panels, blocks[:, 0], axis=0).astype(jnp.float32)
    si_coef = jnp.take(panels, blocks[:, 1], axis=0).astype(jnp.float32)
    quarter = jnp.einsum("trab,tbj->tarj", tiles.astype(jnp.float32), si_coef,
                         precision=lax.Precision.HIGHEST).astype(jnp.bfloat16)
    half = jnp.einsum("tai,tarj->irj", la_coef, quarter.astype(jnp.float32),
                      precision=lax.Precision.HIGHEST)
    return half.astype(jnp.bfloat16)


def reference(integrals, coefficients, tile_blocks, block_owner):
    panels = coefficients.reshape(NSH, SB, NMO)
    flat_tiles = integrals.reshape(N_GRP * N_BLK, KT, R, SB, SB)
    flat_blocks = tile_blocks.reshape(N_GRP * N_BLK, KT, 2)
    half_all = lax.map(lambda pair: one_device((pair[0], pair[1], panels)), (flat_tiles, flat_blocks))
    half_all = half_all.reshape(N_GRP, N_BLK, IJB, IPB, R, NMO)
    source, filled = slot_table(block_owner, N_GRP, CAP)
    picked = jnp.take(half_all, source, axis=2)
    picked = jnp.where(filled[None, None, :, None, None, None], picked, jnp.zeros_like(picked))
    picked = jnp.transpose(picked, (2, 0, 3, 1, 4, 5))
    return picked.reshape(N_GRP * CAP, N_GRP, IPB, N_BLK * R, NMO)
```

```python
import functools
import math

import jax
import jax.numpy as jnp
from jax import lax
from jax.experimental import pallas as pl
from jax.experimental.pallas import tpu as pltpu
from jax.sharding import PartitionSpec as P

NMO = 192
SB = 128
KT = 10
R = 24
IJB = 48
CAP = 24
IPB = 4
LANE = 128
HALF = NMO - LANE
SG = 3
WIDE = CAP * IPB
PACK = WIDE + WIDE // 2
RC = 2
NCH = R // RC
MESH = pl.DeviceIdType.MESH
BF = jnp.bfloat16
F32 = jnp.float32


def exchange(
    n_grp, n_blk, ints, coef, tile_blocks, owner, out,
    iv, table, panels, si, lat, quarter, send,
    int_sem, own_sem, gs_sem, gr_sem, fs_sem, fr_sem, s_sem, r_sem, l_sem,
):
    g = lax.axis_index("grp")
    b = lax.axis_index("blk")
    z = b // 2
    c = b % 2
    sib = z * 2 + (1 - c)
    n_z = n_blk // 2
    depth, unit = coef.shape[0], coef.shape[1]

    load = pltpu.make_async_copy(ints, iv, int_sem)
    load.start()

    def rows(blk):
        return pl.ds(blk * depth, depth)

    keep = pltpu.make_async_copy(coef, table.at[rows(b)], own_sem)
    keep.start()

    barrier = pltpu.get_barrier_semaphore()
    for k in range(1, n_z):
        pl.semaphore_signal(barrier, inc=1, device_id=(g, lax.rem(z + k, n_z) * 2 + c), device_id_type=MESH)
    pl.semaphore_signal(barrier, inc=1, device_id=(g, sib), device_id_type=MESH)
    for k in range(1, n_grp):
        pl.semaphore_signal(barrier, inc=1, device_id=(lax.rem(g + k, n_grp), b), device_id_type=MESH)
    pl.semaphore_wait(barrier, n_z + n_grp - 1)

    far = []
    for k in range(1, n_z):
        far.append(pltpu.make_async_remote_copy(
            src_ref=coef, dst_ref=table.at[rows(b)], send_sem=gs_sem.at[k], recv_sem=gr_sem.at[k],
            device_id=(g, lax.rem(z + k, n_z) * 2 + c), device_id_type=MESH))
        far[-1].start()
    near = [pltpu.make_async_remote_copy(
        src_ref=coef, dst_ref=table.at[rows(b)], send_sem=fs_sem.at[0], recv_sem=fr_sem.at[0],
        device_id=(g, sib), device_id_type=MESH)]
    near[0].start()

    lane = lax.broadcasted_iota(jnp.int32, (8, NMO), 1)
    kl = lane // IPB
    own = jnp.zeros((8, NMO), jnp.int32)
    for k in range(IJB):
        own = jnp.where(kl == k, owner[k], own)
    rank = jnp.zeros((8, NMO), jnp.int32)
    for k in range(IJB):
        rank = rank + jnp.where((own == owner[k]) & (kl > k), 1, 0)
    want = (own * CAP + rank) * IPB + lane % IPB
    row = lax.broadcasted_iota(jnp.int32, (n_grp * WIDE, NMO), 0)
    low = row % 32
    here = ((row // 32) * 8 + (low % 16) // 2) * IPB + (low // 16) * 2 + low % 2
    perm = jnp.where(here == want[0:1, :], 1.0, 0.0).astype(F32).astype(BF)

    for k in range(1, n_z):
        far[k - 1].wait_recv()
        got = rows(lax.rem(z + n_z - k, n_z) * 2 + c)
        near.append(pltpu.make_async_remote_copy(
            src_ref=table.at[got], dst_ref=table.at[got], send_sem=fs_sem.at[k], recv_sem=fr_sem.at[k],
            device_id=(g, sib), device_id_type=MESH))
        near[-1].start()
    keep.wait()
    for k in range(n_z):
        near[k].wait_recv()
    for k in range(1, n_z):
        far[k - 1].wait_send()
    for k in range(n_z):
        near[k].wait_send()

    if unit == SB:
        panels = table
    else:
        each = SB // unit
        for i in range(table.shape[0]):
            panels[i // each, (i % each) * unit:(i % each + 1) * unit, :] = table[i]
    for t in range(KT):
        la = panels[tile_blocks[t, 0]]
        lat[:, t * SB:(t + 1) * SB] = lax.dot_general(
            perm, la, (((1,), (1,)), ((), ())), preferred_element_type=F32).astype(BF)
        si[t] = panels[tile_blocks[t, 1]]
    load.wait()

    def piece(peer, ch, k):
        return pltpu.make_async_remote_copy(
            src_ref=send.at[peer, pl.ds(ch * RC, RC)], dst_ref=out.at[g, pl.ds(ch * RC, RC)],
            send_sem=s_sem.at[k, ch], recv_sem=r_sem.at[k, ch],
            device_id=(peer, b), device_id_type=MESH)

    def mine():
        return pltpu.make_async_copy(send.at[g], out.at[g], l_sem)

    def chunk(ch, carry):
        for u in range(RC):
            r = ch * RC + u
            for t in range(KT):
                quarter[u, t * SB:(t + 1) * SB, :] = jnp.dot(
                    iv[t, r], si[t], preferred_element_type=F32).astype(BF)
            half = jnp.dot(lat[...], quarter[u], preferred_element_type=F32)
            for o in range(n_grp):
                for s in range(SG):
                    at = o * WIDE + s * 32
                    even, odd = half[at:at + 16], half[at + 16:at + 32]
                    send[o, r, s * 48:s * 48 + 16, :] = even[:, :LANE].astype(BF)
                    send[o, r, s * 48 + 16:s * 48 + 32, :] = odd[:, :LANE].astype(BF)
                    send[o, r, s * 48 + 32:s * 48 + 48, :] = jnp.concatenate(
                        [even[:, LANE:], odd[:, LANE:]], axis=1).astype(BF)
        for k in range(1, n_grp):
            piece(lax.rem(g + k, n_grp), ch, k).start()
        return carry

    lax.fori_loop(0, NCH, chunk, 0)
    mine().start()

    def drain(ch, carry):
        for k in range(1, n_grp):
            copy = piece(lax.rem(g + k, n_grp), ch, k)
            copy.wait_send()
            copy.wait_recv()
        return carry

    lax.fori_loop(0, NCH, drain, 0)
    mine().wait()


def unpack(x_ref, o_ref, rows):
    for r in range(R):
        rows[pl.ds(r, 48, stride=R), :] = x_ref[0, r].astype(F32)
    for s in range(8):
        for q in range(2):
            i = s * 2 + q
            tail = rows[pl.ds((32 + i) * R, R), :]
            o_ref[s, 0, q, :, :LANE] = rows[pl.ds(i * R, R), :].astype(BF)
            o_ref[s, 0, 2 + q, :, :LANE] = rows[pl.ds((16 + i) * R, R), :].astype(BF)
            o_ref[s, 0, q, :, LANE:] = tail[:, :HALF].astype(BF)
            o_ref[s, 0, 2 + q, :, LANE:] = tail[:, HALF:].astype(BF)


def body(n_grp, n_blk, integrals, coefficients, tile_blocks, block_owner):
    anyspace = pl.BlockSpec(memory_space=pl.ANY)
    smem = pl.BlockSpec(memory_space=pltpu.SMEM)
    n_z = n_blk // 2
    depth = coefficients.shape[0]
    unit = math.gcd(depth, SB)
    total = n_blk * depth
    packed = pl.pallas_call(
        functools.partial(exchange, n_grp, n_blk),
        out_shape=jax.ShapeDtypeStruct((n_grp, R, PACK, LANE), BF),
        in_specs=[anyspace, pl.BlockSpec(memory_space=pltpu.VMEM), smem, smem],
        out_specs=anyspace,
        scratch_shapes=[
            pltpu.VMEM((KT, R, SB, SB), BF),
            pltpu.VMEM((total // unit, unit, NMO), BF),
            pltpu.VMEM((1 if unit == SB else total // SB, SB, NMO), BF),
            pltpu.VMEM((KT, SB, NMO), BF),
            pltpu.VMEM((n_grp * WIDE, KT * SB), BF),
            pltpu.VMEM((RC, KT * SB, NMO), BF),
            pltpu.VMEM((n_grp, R, PACK, LANE), BF),
            pltpu.SemaphoreType.DMA,
            pltpu.SemaphoreType.DMA,
            pltpu.SemaphoreType.DMA((n_z,)),
            pltpu.SemaphoreType.DMA((n_z,)),
            pltpu.SemaphoreType.DMA((n_z,)),
            pltpu.SemaphoreType.DMA((n_z,)),
            pltpu.SemaphoreType.DMA((n_grp, NCH)),
            pltpu.SemaphoreType.DMA((n_grp, NCH)),
            pltpu.SemaphoreType.DMA,
        ],
        compiler_params=pltpu.CompilerParams(
            collective_id=0, has_side_effects=True, vmem_limit_bytes=40 * 2**20),
    )(integrals[0, 0], coefficients.reshape(depth // unit, unit, NMO), tile_blocks[0, 0], block_owner)
    return pl.pallas_call(
        unpack,
        grid=(n_grp, SG),
        out_shape=jax.ShapeDtypeStruct((CAP, n_grp, IPB, R, NMO), BF),
        in_specs=[pl.BlockSpec((1, R, 48, LANE), lambda g, s: (g, 0, s, 0))],
        out_specs=pl.BlockSpec((8, 1, IPB, R, NMO), lambda g, s: (s, g, 0, 0, 0)),
        scratch_shapes=[pltpu.VMEM((48 * R, LANE), F32)],
        compiler_params=pltpu.CompilerParams(vmem_limit_bytes=40 * 2**20),
    )(packed)


def solution(mesh):
    in_specs = (
        P("grp", "blk", None, None, None, None),
        P("blk", None),
        P("grp", "blk", None, None),
        P(),
    )
    out_specs = P("grp", None, None, "blk", None)
    step = functools.partial(body, mesh.shape["grp"], mesh.shape["blk"])
    return jax.shard_map(step, mesh=mesh, in_specs=in_specs, out_specs=out_specs, check_vma=False)
```

```python
import functools
import math

import jax
import jax.numpy as jnp
from jax import lax
from jax.experimental import pallas as pl
from jax.experimental.pallas import tpu as pltpu
from jax.sharding import PartitionSpec as P

NMO = 192
SB = 128
KT = 10
R = 24
IJB = 48
CAP = 24
IPB = 4
LANE = 128
HALF = NMO - LANE
SG = 3
WIDE = CAP * IPB
PACK = WIDE + WIDE // 2
RC = 2
NCH = R // RC
MESH = pl.DeviceIdType.MESH
BF = jnp.bfloat16
F32 = jnp.float32


def exchange(
    n_grp, n_blk, ints, coef, tile_blocks, owner, out,
    iv, table, panels, si, lat, quarter, send,
    int_sem, own_sem, gs_sem, gr_sem, xs_sem, xr_sem, fs_sem, fr_sem, s_sem, r_sem, l_sem,
):
    g = lax.axis_index("grp")
    b = lax.axis_index("blk")
    z = b // 2
    c = b % 2
    sib = z * 2 + (1 - c)
    n_z = n_blk // 2
    depth, unit = coef.shape[0], coef.shape[1]

    load = pltpu.make_async_copy(ints, iv, int_sem)
    load.start()

    split = unit % (16 * n_grp) == 0
    sub = unit // n_grp if split else unit

    def shard(ref, first, grp):
        part = pl.ds(pl.multiple_of(grp * sub, 16), sub) if split else pl.ds(0, unit)
        return ref.at[pl.ds(first, depth), part]

    def rows(blk):
        return pl.ds(blk * depth, depth)

    keep = pltpu.make_async_copy(coef, table.at[rows(b)], own_sem)
    keep.start()

    barrier = pltpu.get_barrier_semaphore()
    for k in range(1, n_z):
        pl.semaphore_signal(barrier, inc=1, device_id=(g, lax.rem(z + k, n_z) * 2 + c), device_id_type=MESH)
    pl.semaphore_signal(barrier, inc=1, device_id=(g, sib), device_id_type=MESH)
    for k in range(1, n_grp):
        pl.semaphore_signal(barrier, inc=1, device_id=(lax.rem(g + k, n_grp), b), device_id_type=MESH)
    pl.semaphore_wait(barrier, n_z + n_grp - 1)

    far = []
    for k in range(1, n_z):
        far.append(pltpu.make_async_remote_copy(
            src_ref=shard(coef, 0, g), dst_ref=shard(table, b * depth, g),
            send_sem=gs_sem.at[k], recv_sem=gr_sem.at[k],
            device_id=(g, lax.rem(z + k, n_z) * 2 + c), device_id_type=MESH))
        far[-1].start()
    near = [pltpu.make_async_remote_copy(
        src_ref=coef, dst_ref=table.at[rows(b)], send_sem=fs_sem.at[0, 0], recv_sem=fr_sem.at[0, 0],
        device_id=(g, sib), device_id_type=MESH)]
    near[0].start()

    lane = lax.broadcasted_iota(jnp.int32, (8, NMO), 1)
    kl = lane // IPB
    own = jnp.zeros((8, NMO), jnp.int32)
    for k in range(IJB):
        own = jnp.where(kl == k, owner[k], own)
    rank = jnp.zeros((8, NMO), jnp.int32)
    for k in range(IJB):
        rank = rank + jnp.where((own == owner[k]) & (kl > k), 1, 0)
    want = (own * CAP + rank) * IPB + lane % IPB
    row = lax.broadcasted_iota(jnp.int32, (n_grp * WIDE, NMO), 0)
    low = row % 32
    here = ((row // 32) * 8 + (low % 16) // 2) * IPB + (low // 16) * 2 + low % 2
    perm = jnp.where(here == want[0:1, :], 1.0, 0.0).astype(F32).astype(BF)

    def forward(k, j):
        ref = shard(table, (lax.rem(z + n_z - k, n_z) * 2 + c) * depth, lax.rem(g + n_grp - j, n_grp))
        near.append(pltpu.make_async_remote_copy(
            src_ref=ref, dst_ref=ref, send_sem=fs_sem.at[k, j], recv_sem=fr_sem.at[k, j],
            device_id=(g, sib), device_id_type=MESH))
        near[-1].start()

    across = []
    for k in range(1, n_z):
        far[k - 1].wait_recv()
        if split:
            ref = shard(table, (lax.rem(z + n_z - k, n_z) * 2 + c) * depth, g)
            for j in range(1, n_grp):
                across.append(pltpu.make_async_remote_copy(
                    src_ref=ref, dst_ref=ref, send_sem=xs_sem.at[k, j], recv_sem=xr_sem.at[k, j],
                    device_id=(lax.rem(g + j, n_grp), b), device_id_type=MESH))
                across[-1].start()
        forward(k, 0)
    if split:
        for k in range(1, n_z):
            for j in range(1, n_grp):
                across[(k - 1) * (n_grp - 1) + j - 1].wait_recv()
                forward(k, j)
    keep.wait()
    for copy in near:
        copy.wait_recv()
    for copy in far + across + near:
        copy.wait_send()

    if unit == SB:
        panels = table
    else:
        each = SB // unit
        for i in range(table.shape[0]):
            panels[i // each, (i % each) * unit:(i % each + 1) * unit, :] = table[i]
    for t in range(KT):
        la = panels[tile_blocks[t, 0]]
        lat[:, t * SB:(t + 1) * SB] = lax.dot_general(
            perm, la, (((1,), (1,)), ((), ())), preferred_element_type=F32).astype(BF)
        si[t] = panels[tile_blocks[t, 1]]
    load.wait()

    def piece(peer, ch, k):
        return pltpu.make_async_remote_copy(
            src_ref=send.at[peer, pl.ds(ch * RC, RC)], dst_ref=out.at[g, pl.ds(ch * RC, RC)],
            send_sem=s_sem.at[k, ch], recv_sem=r_sem.at[k, ch],
            device_id=(peer, b), device_id_type=MESH)

    def mine():
        return pltpu.make_async_copy(send.at[g], out.at[g], l_sem)

    def chunk(ch, carry):
        for u in range(RC):
            r = ch * RC + u
            for t in range(KT):
                quarter[u, t * SB:(t + 1) * SB, :] = jnp.dot(
                    iv[t, r], si[t], preferred_element_type=F32).astype(BF)
            half = jnp.dot(lat[...], quarter[u], preferred_element_type=F32)
            for o in range(n_grp):
                for s in range(SG):
                    at = o * WIDE + s * 32
                    even, odd = half[at:at + 16], half[at + 16:at + 32]
                    send[o, r, s * 48:s * 48 + 16, :] = even[:, :LANE].astype(BF)
                    send[o, r, s * 48 + 16:s * 48 + 32, :] = odd[:, :LANE].astype(BF)
                    send[o, r, s * 48 + 32:s * 48 + 48, :] = jnp.concatenate(
                        [even[:, LANE:], odd[:, LANE:]], axis=1).astype(BF)
        for k in range(1, n_grp):
            piece(lax.rem(g + k, n_grp), ch, k).start()
        return carry

    lax.fori_loop(0, NCH, chunk, 0)
    mine().start()

    def drain(ch, carry):
        for k in range(1, n_grp):
            copy = piece(lax.rem(g + k, n_grp), ch, k)
            copy.wait_send()
            copy.wait_recv()
        return carry

    lax.fori_loop(0, NCH, drain, 0)
    mine().wait()


def unpack(x_ref, o_ref, rows):
    for r in range(R):
        rows[pl.ds(r, 48, stride=R), :] = x_ref[0, r].astype(F32)
    for s in range(8):
        for q in range(2):
            i = s * 2 + q
            tail = rows[pl.ds((32 + i) * R, R), :]
            o_ref[s, 0, q, :, :LANE] = rows[pl.ds(i * R, R), :].astype(BF)
            o_ref[s, 0, 2 + q, :, :LANE] = rows[pl.ds((16 + i) * R, R), :].astype(BF)
            o_ref[s, 0, q, :, LANE:] = tail[:, :HALF].astype(BF)
            o_ref[s, 0, 2 + q, :, LANE:] = tail[:, HALF:].astype(BF)


def body(n_grp, n_blk, integrals, coefficients, tile_blocks, block_owner):
    hbm = pl.BlockSpec(memory_space=pltpu.HBM)
    smem = pl.BlockSpec(memory_space=pltpu.SMEM)
    n_z = n_blk // 2
    depth = coefficients.shape[0]
    unit = math.gcd(depth, SB)
    total = n_blk * depth
    packed = pl.pallas_call(
        functools.partial(exchange, n_grp, n_blk),
        out_shape=jax.ShapeDtypeStruct((n_grp, R, PACK, LANE), BF),
        in_specs=[hbm, hbm, smem, smem],
        out_specs=hbm,
        scratch_shapes=[
            pltpu.VMEM((KT, R, SB, SB), BF),
            pltpu.VMEM((total // unit, unit, NMO), BF),
            pltpu.VMEM((1 if unit == SB else total // SB, SB, NMO), BF),
            pltpu.VMEM((KT, SB, NMO), BF),
            pltpu.VMEM((n_grp * WIDE, KT * SB), BF),
            pltpu.VMEM((RC, KT * SB, NMO), BF),
            pltpu.VMEM((n_grp, R, PACK, LANE), BF),
            pltpu.SemaphoreType.DMA,
            pltpu.SemaphoreType.DMA,
            pltpu.SemaphoreType.DMA((n_z,)),
            pltpu.SemaphoreType.DMA((n_z,)),
            pltpu.SemaphoreType.DMA((n_z, n_grp)),
            pltpu.SemaphoreType.DMA((n_z, n_grp)),
            pltpu.SemaphoreType.DMA((n_z, n_grp)),
            pltpu.SemaphoreType.DMA((n_z, n_grp)),
            pltpu.SemaphoreType.DMA((n_grp, NCH)),
            pltpu.SemaphoreType.DMA((n_grp, NCH)),
            pltpu.SemaphoreType.DMA,
        ],
        compiler_params=pltpu.CompilerParams(
            collective_id=0, has_side_effects=True, vmem_limit_bytes=40 * 2**20),
    )(integrals[0, 0], coefficients.reshape(depth // unit, unit, NMO), tile_blocks[0, 0], block_owner)
    return pl.pallas_call(
        unpack,
        grid=(n_grp, SG),
        out_shape=jax.ShapeDtypeStruct((CAP, n_grp, IPB, R, NMO), BF),
        in_specs=[pl.BlockSpec((1, R, 48, LANE), lambda g, s: (g, 0, s, 0))],
        out_specs=pl.BlockSpec((8, 1, IPB, R, NMO), lambda g, s: (s, g, 0, 0, 0)),
        scratch_shapes=[pltpu.VMEM((48 * R, LANE), F32)],
        compiler_params=pltpu.CompilerParams(vmem_limit_bytes=40 * 2**20),
    )(packed)


def solution(mesh):
    in_specs = (
        P("grp", "blk", None, None, None, None),
        P("blk", None),
        P("grp", "blk", None, None),
        P(),
    )
    out_specs = P("grp", None, None, "blk", None)
    step = functools.partial(body, mesh.shape["grp"], mesh.shape["blk"])
    return jax.shard_map(step, mesh=mesh, in_specs=in_specs, out_specs=out_specs, check_vma=False)
```
